512 devices in a mesh: img: 64 (over y, z), blk: 8 (over x, core).
Axes of the slice: x: 4, y: 4, z: 16, core: 2. Of those that a mesh axis runs over, the one named last changes fastest.
Arguments:
- descriptors: bfloat16 [1024, 128, 256], P(('img', 'blk')), may hold values from -8 to 8
- covisible: int32 [1024, 6], P(('img', 'blk')), may hold values from 0 to 1023, as said below
- tile_counts: int32 [1024], P(('img', 'blk')), may hold values from 1 to 6, as said below
- keypoints: int32 [1024], replicated, may hold values from 32 to 128, as said below
- query_weight: bfloat16 [256, 256], replicated, may hold values from -0.375 to 0.375
- key_weight: bfloat16 [256, 256], replicated, may hold values from -0.375 to 0.375
- value_weight: bfloat16 [256, 256], replicated, may hold values from -0.375 to 0.375
- merge_weight: bfloat16 [512, 512], replicated, may hold values from -0.25 to 0.25
- output_weight: bfloat16 [512, 256], replicated, may hold values from -0.25 to 0.25
- dustbin: float32 [1], replicated, may hold values from 0.5 to 2
Outputs:
- plan: float32 [1024, 6, 128, 128], P(('img', 'blk'))
- row_bin: float32 [1024, 128], P(('img', 'blk'))
- col_bin: float32 [1024, 128], P(('img', 'blk'))
The draws below stay inside these ranges and needn't reach their ends.
Inputs may be any that keep to these rules, and one draw needn't show every extreme that they name: `covisible`: the 6 entries of a block's row name different blocks, never the block itself, all within its own image group of 16 consecutive blocks or the groups just before and after it. `tile_counts`: some block uses all 6 of its listed blocks. The valid keypoints of a block are its first ones; some block is full.
All inputs are finite; a program needn't handle non-finite values.
Results may differ from the reference program's by a relative error of at most 0.0032.
Values may be sent and summed in bfloat16 or wider, within the bound.
No kernel may reach another device: no remote copies, remote signals or barrier semaphores. Data moves between devices by JAX's collectives and lax.ppermute only.
A program may use at most 64 MiB of HBM per device.

```python
import math
import jax
import jax.numpy as jnp
from jax import lax

D = 256
HEADS = 4
BLOCK = 128
TILES = 6
ITERS = 3
GROUP = 16
NB = 1024


def draw_descriptors(key, part):
    drawn_key = jax.random.fold_in(key, 101)
    return jnp.clip(jax.random.normal(drawn_key, (NB, BLOCK, D), jnp.float32), -8.0, 8.0).astype(jnp.bfloat16)


def draw_covisible(key, part):
    rows = jnp.arange(NB, dtype=jnp.int32)
    groups = rows // GROUP
    slots = jnp.arange(3 * GROUP, dtype=jnp.int32)
    candidate = (groups[:, None] - 1) * GROUP + slots[None, :]
    usable = (candidate >= 0) & (candidate < NB) & (candidate != rows[:, None])
    ranks = jax.vmap(lambda sub: jax.random.permutation(sub, 3 * GROUP))(jax.random.split(jax.random.fold_in(key, 201), NB))
    ranking = ranks.astype(jnp.int32) + jnp.where(usable, 0, 3 * GROUP)
    order = jnp.argsort(ranking, axis=1, stable=True)[:, :TILES]
    return jnp.take_along_axis(candidate, order, axis=1).astype(jnp.int32)


def draw_tile_counts(key, part):
    rows = jnp.arange(NB, dtype=jnp.int32)
    drawn = jax.random.randint(jax.random.fold_in(key, 301), (NB,), 1, TILES + 1)
    return jnp.where(rows % 5 == 0, TILES, drawn).astype(jnp.int32)


def draw_keypoints(key, part):
    rows = jnp.arange(NB, dtype=jnp.int32)
    drawn = jax.random.randint(jax.random.fold_in(key, 401), (NB,), BLOCK // 4, BLOCK + 1)
    return jnp.where(rows % 3 == 0, BLOCK, drawn).astype(jnp.int32)


def normal_values(rng, extent, spread, limit, held_as=jnp.bfloat16):
    return jnp.clip(spread * jax.random.normal(rng, extent, jnp.float32), -limit, limit).astype(held_as)


def setup_inputs(seed: int = 0) -> dict:
    splits = jax.random.split(jax.random.key(seed), 11)
    return {
        "descriptors": draw_descriptors(jax.random.fold_in(splits[10], 71), 0),
        "covisible": draw_covisible(jax.random.fold_in(splits[10], 71), 0),
        "tile_counts": draw_tile_counts(jax.random.fold_in(splits[10], 71), 0),
        "keypoints": draw_keypoints(jax.random.fold_in(splits[10], 71), 0),
        "query_weight": normal_values(splits[4], (D, D), D ** -0.5, 0.375),
        "key_weight": normal_values(splits[5], (D, D), D ** -0.5, 0.375),
        "value_weight": normal_values(splits[6], (D, D), D ** -0.5, 0.375),
        "merge_weight": normal_values(splits[7], (2 * D, 2 * D), (2 * D) ** -0.5, 0.25),
        "output_weight": normal_values(splits[8], (2 * D, D), (2 * D) ** -0.5, 0.25),
        "dustbin": jnp.clip(jax.random.uniform(splits[9], (1,), jnp.float32, 0.5, 2.0), 0.5, 2.0),
    }


def project_rows(values, weight):
    flat = jnp.dot(values.reshape(-1, values.shape[-1]), weight, preferred_element_type=jnp.float32)
    return flat.reshape(values.shape[:-1] + (weight.shape[1],)).astype(jnp.bfloat16)

def reference(descriptors, covisible, tile_counts, keypoints, query_weight, key_weight, value_weight, merge_weight, output_weight, dustbin):
    block_count, block_len, feature_dim = descriptors.shape
    head_dim = feature_dim // HEADS
    tile_count = covisible.shape[1]
    query = project_rows(descriptors, query_weight)
    keys_all = project_rows(descriptors, key_weight)
    values_all = project_rows(descriptors, value_weight)
    tile_slots = jnp.arange(tile_count, dtype=jnp.int32)
    positions = jnp.arange(block_len, dtype=jnp.int32)

    def attend(pieces):
        query_block, own_block, row_cols, count = pieces
        key_tiles = keys_all[row_cols].reshape(tile_count * block_len, HEADS, head_dim).astype(jnp.float32)
        value_tiles = values_all[row_cols].reshape(tile_count * block_len, HEADS, head_dim).astype(jnp.float32)
        key_live = (tile_slots[:, None] < count) & (positions[None, :] < keypoints[row_cols][:, None])
        logits = jnp.einsum('qhd,khd->hqk', query_block.reshape(block_len, HEADS, head_dim).astype(jnp.float32), key_tiles) / math.sqrt(head_dim)
        logits = jnp.where(key_live.reshape(1, 1, -1), logits, -1e+30)
        highest = lax.optimization_barrier(jnp.max(logits, axis=2, keepdims=True))
        weights = jnp.exp(logits - highest)
        weights = (weights / lax.optimization_barrier(jnp.sum(weights, axis=2, keepdims=True))).astype(jnp.bfloat16)
        message = jnp.einsum('hqk,khd->qhd', weights.astype(jnp.float32), value_tiles).reshape(block_len, feature_dim).astype(jnp.bfloat16)
        joined = jnp.concatenate([own_block, message], axis=1)
        hidden = jnp.maximum(jnp.dot(joined, merge_weight, preferred_element_type=jnp.float32), 0.0).astype(jnp.bfloat16)
        return (own_block.astype(jnp.float32) + jnp.dot(hidden, output_weight, preferred_element_type=jnp.float32)).astype(jnp.bfloat16)
    refined = lax.map(attend, (query, descriptors, covisible, tile_counts))

    def score_tiles(pieces):
        own_block, row_cols = pieces
        other = refined[row_cols].astype(jnp.float32)
        return jnp.einsum('id,kjd->kij', own_block.astype(jnp.float32), other) / math.sqrt(feature_dim)
    scores = lax.map(score_tiles, (refined, covisible))
    row_live = positions[None, :] < keypoints[:, None]
    tile_live = tile_slots[None, :] < tile_counts[:, None]
    col_live = row_live[covisible]
    valid = tile_live[:, :, None, None] & row_live[:, None, :, None] & col_live[:, :, None, :]
    dust = dustbin[0]
    col_pot = jnp.zeros((block_count, block_len), jnp.float32)
    row_pot = jnp.zeros((block_count, block_len), jnp.float32)
    for sweep in range(ITERS):
        tile_pot = col_pot[covisible]
        shifted = jnp.where(valid, scores + tile_pot[:, :, None, :], -1e+30)
        highest = jnp.maximum(lax.optimization_barrier(jnp.max(shifted, axis=(1, 3))), dust)
        total = lax.optimization_barrier(jnp.sum(jnp.exp(shifted - highest[:, None, :, None]), axis=(1, 3))) + jnp.exp(dust - highest)
        row_pot = -(highest + jnp.log(total))
        mass = lax.optimization_barrier(jnp.sum(jnp.where(valid, jnp.exp(scores + row_pot[:, None, :, None] + tile_pot[:, :, None, :]), 0.0), axis=2))
        col_sum = jax.ops.segment_sum(mass.reshape(block_count * tile_count, block_len), covisible.reshape(-1), num_segments=block_count)
        col_pot = col_pot - jnp.log(col_sum + jnp.exp(dust + col_pot))
    tile_pot = col_pot[covisible]
    plan = jnp.where(valid, scores + row_pot[:, None, :, None] + tile_pot[:, :, None, :], 0.0)
    row_bin = jnp.where(row_live, dust + row_pot, 0.0)
    col_bin = jnp.where(row_live, dust + col_pot, 0.0)
    return (plan, row_bin, col_bin)
```

```python
import functools

import jax
import jax.numpy as jnp
from jax import lax
from jax.experimental import pallas as pl
from jax.experimental.pallas import tpu as pltpu
from jax.sharding import PartitionSpec as P

HEADS = 4
ITERS = 3
BLOCK = 128
D = 256
TILES = 6
GROUP = 16
NEAR = 3 * GROUP
CHUNK = 2 * BLOCK + 16
VMEM = pltpu.VMEM
SMEM = pltpu.SMEM
BF = jnp.bfloat16
F32 = jnp.float32
NT = (((1,), (1,)), ((), ()))


def dot(a, b, dims=(((1,), (0,)), ((), ()))):
    return lax.dot_general(a, b, dims, preferred_element_type=F32)


def lanes(shape):
    return lax.broadcasted_iota(jnp.int32, shape, len(shape) - 1)


def place_of(n, img):
    group = n // GROUP
    j = n % GROUP
    parity = (img + group + 1) % 2
    in_pair = jnp.logical_or(group == 1, group == 2 - 2 * (img % 2))
    chunk = j // 4 + jnp.where(in_pair, 4 * parity, 0)
    return in_pair, (j // 2) % 2, chunk, (j % 2) * BLOCK


def attend_kernel(
    cov_ref, count_ref, kpt_ref, desc_ref, ra, rao, rb, rbo,
    wq_ref, wk_ref, wv_ref, wm_ref, wo_ref, out_ref, tiles, logits, probs,
):
    img = lax.axis_index("img")
    core = lax.axis_index("blk") % 2
    first = (img - 1) * GROUP
    for r in range(2):
        for t in range(TILES):
            n = cov_ref[r, t] - first
            in_pair, its_core, chunk, row = place_of(n, img)
            same = its_core == core
            dst = pl.ds((r * TILES + t) * BLOCK, BLOCK)
            for src, hit in (
                (ra, in_pair & same),
                (rao, in_pair & ~same),
                (rb, ~in_pair & same),
                (rbo, ~in_pair & ~same),
            ):
                @pl.when(hit)
                def _(src=src):
                    tiles[dst, :] = src[chunk, pl.ds(pl.multiple_of(row, BLOCK), BLOCK), :]

    desc = desc_ref[...]
    query = dot(desc, wq_ref[...]).astype(BF) * jnp.asarray(0.125, BF)
    messages = []
    head_of = lanes((BLOCK, D)) // (D // HEADS)
    for r in range(2):
        keys = tiles[pl.ds(r * TILES * BLOCK, TILES * BLOCK), :]
        k = dot(keys, wk_ref[...]).astype(BF)
        v = dot(keys, wv_ref[...]).astype(BF)
        q = query[r * BLOCK : (r + 1) * BLOCK]
        q4 = jnp.concatenate(
            [jnp.where(head_of == h, q, jnp.zeros_like(q)) for h in range(HEADS)], axis=0
        )
        logits[...] = dot(q4, k, NT)
        live = jnp.concatenate(
            [
                lanes((1, BLOCK))
                < jnp.where(t < count_ref[r], kpt_ref[cov_ref[r, t]], 0)
                for t in range(TILES)
            ],
            axis=1,
        )
        for h in range(HEADS):
            rows = pl.ds(h * BLOCK, BLOCK)
            s = jnp.where(live, logits[rows, :], -1e30)
            top = jnp.max(s, axis=1, keepdims=True)
            e = jnp.exp(s - top)
            total = jnp.sum(e, axis=1, keepdims=True)
            probs[rows, :] = (e * (1.0 / total)).astype(BF)
        mixed = dot(probs[...], v)
        message = jnp.zeros((BLOCK, D), F32)
        for h in range(HEADS):
            message = jnp.where(head_of == h, mixed[h * BLOCK : (h + 1) * BLOCK], message)
        messages.append(message.astype(BF))
    message = jnp.concatenate(messages, axis=0)
    hidden = dot(desc, wm_ref[:D, :]) + dot(message, wm_ref[D:, :])
    hidden = jnp.maximum(hidden, 0.0).astype(BF)
    refined = (desc.astype(F32) + dot(hidden, wo_ref[...])).astype(BF)
    for c in range(8):
        out_ref[c] = refined


def row_block(x, k, cov_ref, kpt_ref, blk):
    chip = x // 2
    other = x % 2
    its_core = (blk + other) % 2
    return chip * 4 + its_core * 2 + k


def table(cov_ref, j, t):
    return cov_ref[j * 8 + t]


def column_pass(keep, sums, cov_ref, j, w):
    for t in range(TILES):
        n = table(cov_ref, j, t)
        part = (keep[j * TILES + t] * w).reshape(BLOCK // 8, 8, BLOCK)
        sums[n] += jnp.sum(part, axis=0)


def send_out(sums, core, s_ref, m_ref, f_ref):
    s_ref[...] = jnp.sum(sums[...], axis=1)
    m_ref[...] = s_ref[pl.ds(pl.multiple_of(GROUP * (1 - core), GROUP), 2 * GROUP), :]
    f_ref[...] = s_ref[pl.ds(pl.multiple_of(2 * GROUP * (1 - core), GROUP), GROUP), :]


def build_kernel(
    cov_ref, kpt_ref, dust_ref, ra, rao, rb, rbo,
    keep, top_ref, own_ref, s_ref, m_ref, f_ref, near, sums, raw,
):
    img = lax.axis_index("img")
    blk = lax.axis_index("blk")
    core = blk % 2
    first = (img - 1) * GROUP
    dust = dust_ref[0]
    e = img % 2
    for src, other in ((ra, 0), (rao, 1)):
        for chunk in range(8):
            group = jnp.where(e == 0, 1 + chunk // 4, chunk // 4)
            for k in range(2):
                n = group * GROUP + (chunk % 4) * 4 + ((core + other) % 2) * 2 + k
                near[n] = src[chunk, k * BLOCK : (k + 1) * BLOCK, :]
    for src, other in ((rb, 0), (rbo, 1)):
        for chunk in range(4):
            group = jnp.where(e == 0, 0, 2)
            for k in range(2):
                n = group * GROUP + chunk * 4 + ((core + other) % 2) * 2 + k
                near[n] = src[chunk, k * BLOCK : (k + 1) * BLOCK, :]
    sums[...] = jnp.zeros_like(sums)

    def limit(j, t):
        n = table(cov_ref, j, t)
        return jnp.where(t < table(cov_ref, j, TILES), kpt_ref[first + n], 0)

    def body(j, _):
        mine = near[GROUP + j]
        top = jnp.full((BLOCK, BLOCK), dust, F32)
        for t in range(TILES):
            s = dot(mine, near[table(cov_ref, j, t)], NT) * 0.0625
            s = jnp.where(lanes((BLOCK, BLOCK)) < limit(j, t), s, -1e30)
            raw[t] = s
            top = jnp.maximum(top, s)
        top = jnp.max(top, axis=1, keepdims=True)
        top_ref[j] = jnp.broadcast_to(top, (BLOCK, BLOCK))
        total = jnp.zeros((BLOCK, BLOCK), F32)
        for t in range(TILES):
            k = jnp.exp(raw[t] - top)
            keep[j * TILES + t] = k
            total = total + k
        total = jnp.sum(total, axis=1, keepdims=True) + jnp.exp(dust - top)
        live = lax.broadcasted_iota(jnp.int32, (BLOCK, 1), 0) < kpt_ref[first + GROUP + j]
        w = jnp.broadcast_to(jnp.where(live, 1.0 / total, 0.0), (BLOCK, BLOCK))
        column_pass(keep, sums, cov_ref, j, w)
        return _

    lax.fori_loop(0, GROUP, body, 0)
    for r in range(2):
        j = 2 * blk + r
        for t in range(TILES):
            own_ref[r * TILES + t] = (
                dot(near[GROUP + j], near[table(cov_ref, j, t)], NT) * 0.0625
            )
    send_out(sums, core, s_ref, m_ref, f_ref)


def column_total(core, s_ref, x_ref, y_ref, total):
    total[...] = s_ref[...]
    for ref, c in ((x_ref, core), (y_ref, 1 - core)):
        at = pl.multiple_of(GROUP * c, GROUP)
        total[pl.ds(at, 2 * GROUP), :] += ref[: 2 * GROUP, :]
        at = pl.multiple_of(2 * GROUP * c, GROUP)
        total[pl.ds(at, GROUP), :] += ref[2 * GROUP :, :]


def sweep_kernel(
    last, cov_ref, kpt_ref, dust_ref, keep, top_ref, own_ref, s_in, x_ref, y_ref, *refs
):
    if last:
        s_ref, m_ref, f_ref, base_ref, bin_ref, total, scale, sums = refs
    else:
        s_ref, m_ref, f_ref, total, scale, sums = refs
    img = lax.axis_index("img")
    blk = lax.axis_index("blk")
    core = blk % 2
    first = (img - 1) * GROUP
    dust = dust_ref[0]
    column_total(core, s_in, x_ref, y_ref, total)
    v = 1.0 / (total[...] + jnp.exp(jnp.full((NEAR, BLOCK), dust, F32)))
    scale[...] = jnp.broadcast_to(v[:, None, :], (NEAR, 8, BLOCK))
    sums[...] = jnp.zeros_like(sums)

    def row_total(j):
        part = jnp.zeros((BLOCK // 8, 8, BLOCK), F32)
        for t in range(TILES):
            k = keep[j * TILES + t].reshape(BLOCK // 8, 8, BLOCK)
            part = part + k * scale[table(cov_ref, j, t)][None]
        part = jnp.sum(part.reshape(BLOCK, BLOCK), axis=1, keepdims=True)
        return part + jnp.exp(dust - top_ref[j])

    def body(j, _):
        live = lax.broadcasted_iota(jnp.int32, (BLOCK, BLOCK), 0) < kpt_ref[first + GROUP + j]
        w = jnp.where(live, 1.0 / row_total(j), 0.0)
        column_pass(keep, sums, cov_ref, j, w)
        return _

    lax.fori_loop(0, GROUP, body, 0)
    send_out(sums, core, s_ref, m_ref, f_ref)
    if last:
        eye = lax.broadcasted_iota(jnp.int32, (BLOCK, BLOCK), 0) == lanes((BLOCK, BLOCK))
        for r in range(2):
            j = 2 * blk + r
            row_pot = -(top_ref[j] + jnp.log(row_total(j)))
            for t in range(TILES):
                base_ref[r * TILES + t] = own_ref[r * TILES + t] + row_pot
            flat = jnp.sum(jnp.where(eye, row_pot, 0.0), axis=0, keepdims=True)
            bin_ref[r : r + 1, :] = jnp.where(
                lanes((1, BLOCK)) < kpt_ref[first + GROUP + j], dust + flat, 0.0
            )


def plan_kernel(
    cov_ref, kpt_ref, dust_ref, base_ref, s_in, x_ref, y_ref, plan_hbm, bin_ref, total, pots, plan, sems
):
    img = lax.axis_index("img")
    blk = lax.axis_index("blk")
    first = (img - 1) * GROUP
    dust = dust_ref[0]
    column_total(blk % 2, s_in, x_ref, y_ref, total)
    pot = -jnp.log(total[...] + jnp.exp(jnp.full((NEAR, BLOCK), dust, F32)))
    total[...] = pot
    pots[...] = jnp.broadcast_to(pot[:, None, :], (NEAR, 8, BLOCK))
    copies = []
    for r in range(2):
        j = 2 * blk + r
        rows = lax.broadcasted_iota(jnp.int32, (BLOCK, BLOCK), 0) < kpt_ref[first + GROUP + j]
        for t in range(TILES):
            n = table(cov_ref, j, t)
            limit = jnp.where(t < table(cov_ref, j, TILES), kpt_ref[first + n], 0)
            full = base_ref[r * TILES + t].reshape(BLOCK // 8, 8, BLOCK) + pots[n][None]
            plan[r, t] = jnp.where(
                rows & (lanes((BLOCK, BLOCK)) < limit), full.reshape(BLOCK, BLOCK), 0.0
            )
            copy = pltpu.make_async_copy(
                plan.at[r, t], plan_hbm.at[r, t], sems.at[r * TILES + t]
            )
            copy.start()
            copies.append(copy)
        own = total[pl.ds(GROUP + j, 1), :]
        bin_ref[r : r + 1, :] = jnp.where(
            lanes((1, BLOCK)) < kpt_ref[first + GROUP + j], dust + own, 0.0
        )
    for copy in copies:
        copy.wait()


def swap_cores(x):
    count = lax.axis_size("blk")
    return lax.ppermute(x, "blk", [(b, b ^ 1) for b in range(count)])


def outwards(x, distance):
    imgs, blks = lax.axis_size("img"), lax.axis_size("blk")
    route = []
    for i in range(imgs):
        for b in range(blks):
            to = i + distance * (1 - 2 * (b % 2))
            if 0 <= to < imgs:
                route.append((i * blks + b, to * blks + b))
    return lax.ppermute(x, ("img", "blk"), route)


def pairs(offset):
    imgs, blks = lax.axis_size("img"), lax.axis_size("blk")
    groups = []
    for i in range(offset, imgs + offset, 2):
        for c in range(2):
            groups.append([(k % imgs) * blks + b for k in (i, i + 1) for b in range(c, blks, 2)])
    return groups


def gather_near(copies):
    ra = lax.all_to_all(
        copies, ("img", "blk"), 0, 0, tiled=True, axis_index_groups=pairs(0)
    )
    rao = swap_cores(ra)
    rb = lax.all_to_all(
        copies, ("img", "blk"), 0, 0, tiled=True, axis_index_groups=pairs(1)
    )
    e = lax.axis_index("img") % 2
    rb = lax.dynamic_slice_in_dim(rb, 4 * e, 4, axis=0)
    rbo = swap_cores(rb)
    return ra, rao, rb, rbo


def spread(m, f):
    x = jnp.concatenate([outwards(m, 1), outwards(f, 2)], axis=0)
    return x, swap_cores(x)


def call(kernel, ins, outs, scratch, limit):
    spaces = {"s": SMEM, "v": VMEM, "h": pl.ANY}
    out_specs = [pl.BlockSpec(memory_space=spaces[k]) for k, *_ in outs]
    return pl.pallas_call(
        kernel,
        in_specs=[pl.BlockSpec(memory_space=spaces[k]) for k, _ in ins],
        out_specs=out_specs,
        out_shape=[jax.ShapeDtypeStruct(s, d) for _, s, d in outs],
        scratch_shapes=scratch,
        compiler_params=pltpu.CompilerParams(vmem_limit_bytes=limit << 20),
    )(*[a for _, a in ins])


def on_device(
    descriptors, covisible, tile_counts, keypoints,
    query_weight, key_weight, value_weight, merge_weight, output_weight, dustbin,
):
    img = lax.axis_index("img")
    blk = lax.axis_index("blk")
    flat = descriptors.reshape(2 * BLOCK, D)
    lists = jnp.concatenate([covisible - (img - 1) * GROUP, tile_counts[:, None]], axis=1)
    lists = jnp.pad(lists.astype(BF), ((0, 14), (0, D - TILES - 1)))
    sent = jnp.concatenate([flat, lists], axis=0)
    sent = jnp.broadcast_to(sent[None], (8, CHUNK, D))
    ra, rao, rb, rbo = gather_near(sent)

    (refined,) = call(
        attend_kernel,
        [("s", covisible), ("s", tile_counts), ("s", keypoints), ("v", flat)]
        + [("v", a) for a in (ra, rao, rb, rbo)]
        + [("v", a) for a in (query_weight, key_weight, value_weight, merge_weight, output_weight)],
        [("v", (8, 2 * BLOCK, D), BF)],
        [
            VMEM((2 * TILES * BLOCK, D), BF),
            VMEM((HEADS * BLOCK, TILES * BLOCK), F32),
            VMEM((HEADS * BLOCK, TILES * BLOCK), BF),
        ],
        24,
    )

    e = img % 2
    mine = lax.dynamic_slice(ra, (4 * e, 2 * BLOCK, 0), (4, 2, 8))
    other = lax.dynamic_slice(rao, (4 * e, 2 * BLOCK, 0), (4, 2, 8))
    core = blk % 2
    lists = jnp.where(
        core == 0, jnp.stack([mine, other], axis=1), jnp.stack([other, mine], axis=1)
    )
    lists = lists.astype(F32).astype(jnp.int32).reshape(GROUP * 8)
    smem = [("s", lists), ("s", keypoints), ("s", dustbin)]

    near = gather_near(refined)
    sums = [("v", (NEAR, BLOCK), F32), ("v", (2 * GROUP, BLOCK), F32), ("v", (GROUP, BLOCK), F32)]
    tile = (BLOCK, BLOCK)
    keep, top, own, s, m, f = call(
        build_kernel,
        smem + [("v", a) for a in near],
        [("v", (GROUP * TILES, *tile), F32), ("v", (GROUP, *tile), F32), ("v", (2 * TILES, *tile), F32)]
        + sums,
        [VMEM((NEAR, BLOCK, D), BF), VMEM((NEAR, 8, BLOCK), F32), VMEM((TILES, *tile), F32)],
        24,
    )
    for sweep in range(1, ITERS):
        x, y = spread(m, f)
        last = sweep == ITERS - 1
        more = [("v", (2 * TILES, *tile), F32), ("v", (2, BLOCK), F32)] if last else []
        got = call(
            functools.partial(sweep_kernel, last),
            smem + [("v", a) for a in (keep, top, own, s, x, y)],
            sums + more,
            [VMEM((NEAR, BLOCK), F32), VMEM((NEAR, 8, BLOCK), F32), VMEM((NEAR, 8, BLOCK), F32)],
            16,
        )
        s, m, f = got[:3]
    base, row_bin = got[3:]
    x, y = spread(m, f)
    plan, col_bin = call(
        plan_kernel,
        smem + [("v", a) for a in (base, s, x, y)],
        [("h", (2, TILES, *tile), F32), ("v", (2, BLOCK), F32)],
        [
            VMEM((NEAR, BLOCK), F32),
            VMEM((NEAR, 8, BLOCK), F32),
            VMEM((2, TILES, *tile), F32),
            pltpu.SemaphoreType.DMA((2 * TILES,)),
        ],
        16,
    )
    return plan, row_bin, col_bin


def solution(mesh):
    split = P(("img", "blk"))
    in_specs = (split, split, split, P(), P(), P(), P(), P(), P(), P())
    return jax.shard_map(
        on_device, mesh=mesh, in_specs=in_specs, out_specs=(split, split, split), check_vma=False
    )
```

```python
import functools

import jax
import jax.numpy as jnp
from jax import lax
from jax.experimental import pallas as pl
from jax.experimental.pallas import tpu as pltpu
from jax.sharding import PartitionSpec as P

HEADS = 4
ITERS = 3
BLOCK = 128
D = 256
TILES = 6
GROUP = 16
NEAR = 3 * GROUP
CHUNK = 2 * BLOCK + 16
VMEM = pltpu.VMEM
SMEM = pltpu.SMEM
BF = jnp.bfloat16
F32 = jnp.float32
NT = (((1,), (1,)), ((), ()))


def dot(a, b, dims=(((1,), (0,)), ((), ()))):
    return lax.dot_general(a, b, dims, preferred_element_type=F32)


def lanes(shape):
    return lax.broadcasted_iota(jnp.int32, shape, len(shape) - 1)


def pack_kernel(cov_ref, count_ref, desc_ref, out_ref):
    first = (lax.axis_index("img") - 1) * GROUP
    rows = lax.broadcasted_iota(jnp.int32, (16, D), 0)
    at = lanes((16, D))
    lists = jnp.zeros((16, D), F32)
    for r in range(2):
        for t in range(TILES + 1):
            value = count_ref[r] if t == TILES else cov_ref[r, t] - first
            lists = jnp.where((rows == r) & (at == t), value.astype(F32), lists)
    for c in range(4):
        out_ref[c, : 2 * BLOCK, :] = desc_ref[...]
        out_ref[c, 2 * BLOCK :, :] = lists.astype(BF)


def attend_kernel(
    cov_ref, count_ref, kpt_ref, desc_ref, own, own_o, low, low_o, high, high_o,
    wq_ref, wk_ref, wv_ref, wm_ref, wo_ref, out_ref, lists_ref, tiles, logits, probs,
):
    img = lax.axis_index("img")
    core = lax.axis_index("blk") % 2
    first = (img - 1) * GROUP
    for src, its_core in ((own, core), (own_o, 1 - core)):
        for x in range(4):
            lists = src[x, 2 * BLOCK :, :BLOCK].astype(F32).astype(jnp.int32)
            lists_ref[pl.ds(4 * x + 2 * its_core, 2), :] = lists[:2]
    for r in range(2):
        for t in range(TILES):
            n = cov_ref[r, t] - first
            group, chip, row = n // GROUP, n % GROUP // 4, n % 2 * BLOCK
            same = n // 2 % 2 == core
            dst = pl.ds((r * TILES + t) * BLOCK, BLOCK)
            for g, pair in enumerate(((low, low_o), (own, own_o), (high, high_o))):
                for src, hit in zip(pair, (same, ~same)):
                    @pl.when((group == g) & hit)
                    def _(src=src):
                        tiles[dst, :] = src[chip, pl.ds(pl.multiple_of(row, BLOCK), BLOCK), :]

    desc = desc_ref[...]
    query = dot(desc, wq_ref[...]).astype(BF) * jnp.asarray(0.125, BF)
    messages = []
    head_of = lanes((BLOCK, D)) // (D // HEADS)
    for r in range(2):
        keys = tiles[pl.ds(r * TILES * BLOCK, TILES * BLOCK), :]
        k = dot(keys, wk_ref[...]).astype(BF)
        v = dot(keys, wv_ref[...]).astype(BF)
        q = query[r * BLOCK : (r + 1) * BLOCK]
        q4 = jnp.concatenate(
            [jnp.where(head_of == h, q, jnp.zeros_like(q)) for h in range(HEADS)], axis=0
        )
        logits[...] = dot(q4, k, NT)
        live = jnp.concatenate(
            [
                lanes((1, BLOCK))
                < jnp.where(t < count_ref[r], kpt_ref[cov_ref[r, t]], 0)
                for t in range(TILES)
            ],
            axis=1,
        )
        for h in range(HEADS):
            rows = pl.ds(h * BLOCK, BLOCK)
            s = jnp.where(live, logits[rows, :], -1e30)
            top = jnp.max(s, axis=1, keepdims=True)
            e = jnp.exp(s - top)
            total = jnp.sum(e, axis=1, keepdims=True)
            probs[rows, :] = (e * (1.0 / total)).astype(BF)
        mixed = dot(probs[...], v)
        message = jnp.zeros((BLOCK, D), F32)
        for h in range(HEADS):
            message = jnp.where(head_of == h, mixed[h * BLOCK : (h + 1) * BLOCK], message)
        messages.append(message.astype(BF))
    message = jnp.concatenate(messages, axis=0)
    hidden = dot(desc, wm_ref[:D, :]) + dot(message, wm_ref[D:, :])
    hidden = jnp.maximum(hidden, 0.0).astype(BF)
    refined = (desc.astype(F32) + dot(hidden, wo_ref[...])).astype(BF)
    for c in range(4):
        out_ref[c] = refined


def table(lists_ref, j, t):
    return lists_ref[j, t]


def column_pass(keep, sums, cov_ref, j, w):
    for t in range(TILES):
        n = table(cov_ref, j, t)
        part = (keep[j * TILES + t] * w).reshape(BLOCK // 8, 8, BLOCK)
        sums[n] += jnp.sum(part, axis=0)


def rank(img, core):
    return (img + 2 * core) % 4


def send_out(sums, flat, s_ref, m_ref):
    s = jnp.sum(sums[...], axis=1)
    s_ref[...] = s
    flat[:NEAR, :] = s
    me = rank(lax.axis_index("img"), lax.axis_index("blk") % 2)
    for k in range(4):
        ahead = jnp.clip(k - me, 0, 2)
        m_ref[k] = flat[pl.ds(pl.multiple_of(GROUP * ahead, GROUP), 2 * GROUP), :]


def column_total(s_ref, x_ref, y_ref, total):
    img = lax.axis_index("img")
    total[...] = s_ref[...]
    for ref, core in ((x_ref, lax.axis_index("blk") % 2), (y_ref, 1 - lax.axis_index("blk") % 2)):
        me = rank(img, core)
        for side, there in ((1, me < 2), (-1, me >= 2)):
            near_at, far_at = (GROUP, 2 * GROUP) if side > 0 else (0, 0)

            @pl.when(there & (img + side >= 0) & (img + side < lax.axis_size("img")))
            def _():
                total[near_at : near_at + 2 * GROUP, :] += ref[me + side]

            @pl.when(there & (img + 2 * side >= 0) & (img + 2 * side < lax.axis_size("img")))
            def _():
                total[far_at : far_at + GROUP, :] += ref[me + 2 * side, :GROUP, :]


def build_kernel(
    cov_ref, kpt_ref, dust_ref, own, own_o, low, low_o, high, high_o,
    keep, top_ref, own_ref, s_ref, m_ref, near, sums, flat, raw,
):
    img = lax.axis_index("img")
    blk = lax.axis_index("blk")
    core = blk % 2
    first = (img - 1) * GROUP
    dust = dust_ref[0]
    for g, pair in enumerate(((low, low_o), (own, own_o), (high, high_o))):
        for src, its_core in zip(pair, (core, 1 - core)):
            for x in range(4):
                for k in range(2):
                    near[GROUP * g + 4 * x + 2 * its_core + k] = src[x, k * BLOCK : (k + 1) * BLOCK, :]
    sums[...] = jnp.zeros_like(sums)

    def limit(j, t):
        n = table(cov_ref, j, t)
        return jnp.where(t < table(cov_ref, j, TILES), kpt_ref[first + n], 0)

    def body(j, _):
        mine = near[GROUP + j]
        top = jnp.full((BLOCK, BLOCK), dust, F32)
        for t in range(TILES):
            s = dot(mine, near[table(cov_ref, j, t)], NT) * 0.0625
            s = jnp.where(lanes((BLOCK, BLOCK)) < limit(j, t), s, -1e30)
            raw[t] = s
            top = jnp.maximum(top, s)
        top = jnp.max(top, axis=1, keepdims=True)
        top_ref[j] = jnp.broadcast_to(top, (BLOCK, BLOCK))
        total = jnp.zeros((BLOCK, BLOCK), F32)
        for t in range(TILES):
            k = jnp.exp(raw[t] - top)
            keep[j * TILES + t] = k
            total = total + k
        total = jnp.sum(total, axis=1, keepdims=True) + jnp.exp(dust - top)
        live = lax.broadcasted_iota(jnp.int32, (BLOCK, 1), 0) < kpt_ref[first + GROUP + j]
        w = jnp.broadcast_to(jnp.where(live, 1.0 / total, 0.0), (BLOCK, BLOCK))
        column_pass(keep, sums, cov_ref, j, w)
        return _

    lax.fori_loop(0, GROUP, body, 0)
    for r in range(2):
        j = 2 * blk + r
        for t in range(TILES):
            own_ref[r * TILES + t] = (
                dot(near[GROUP + j], near[table(cov_ref, j, t)], NT) * 0.0625
            )
    send_out(sums, flat, s_ref, m_ref)


def sweep_kernel(
    last, cov_ref, kpt_ref, dust_ref, keep, top_ref, own_ref, s_in, x_ref, y_ref, *refs
):
    if last:
        s_ref, m_ref, base_ref, bin_ref, total, scale, sums, flat = refs
    else:
        s_ref, m_ref, total, scale, sums, flat = refs
    img = lax.axis_index("img")
    blk = lax.axis_index("blk")
    first = (img - 1) * GROUP
    dust = dust_ref[0]
    column_total(s_in, x_ref, y_ref, total)
    v = 1.0 / (total[...] + jnp.exp(jnp.full((NEAR, BLOCK), dust, F32)))
    scale[...] = jnp.broadcast_to(v[:, None, :], (NEAR, 8, BLOCK))
    sums[...] = jnp.zeros_like(sums)

    def row_total(j):
        part = jnp.zeros((BLOCK // 8, 8, BLOCK), F32)
        for t in range(TILES):
            k = keep[j * TILES + t].reshape(BLOCK // 8, 8, BLOCK)
            part = part + k * scale[table(cov_ref, j, t)][None]
        part = jnp.sum(part.reshape(BLOCK, BLOCK), axis=1, keepdims=True)
        return part + jnp.exp(dust - top_ref[j])

    def body(j, _):
        live = lax.broadcasted_iota(jnp.int32, (BLOCK, BLOCK), 0) < kpt_ref[first + GROUP + j]
        w = jnp.where(live, 1.0 / row_total(j), 0.0)
        column_pass(keep, sums, cov_ref, j, w)
        return _

    lax.fori_loop(0, GROUP, body, 0)
    send_out(sums, flat, s_ref, m_ref)
    if last:
        eye = lax.broadcasted_iota(jnp.int32, (BLOCK, BLOCK), 0) == lanes((BLOCK, BLOCK))
        for r in range(2):
            j = 2 * blk + r
            row_pot = -(top_ref[j] + jnp.log(row_total(j)))
            for t in range(TILES):
                base_ref[r * TILES + t] = own_ref[r * TILES + t] + row_pot
            flat = jnp.sum(jnp.where(eye, row_pot, 0.0), axis=0, keepdims=True)
            bin_ref[r : r + 1, :] = jnp.where(
                lanes((1, BLOCK)) < kpt_ref[first + GROUP + j], dust + flat, 0.0
            )


def plan_kernel(
    cov_ref, kpt_ref, dust_ref, base_ref, s_in, x_ref, y_ref, plan_hbm, bin_ref, total, pots, plan, sems
):
    img = lax.axis_index("img")
    blk = lax.axis_index("blk")
    first = (img - 1) * GROUP
    dust = dust_ref[0]
    column_total(s_in, x_ref, y_ref, total)
    pot = -jnp.log(total[...] + jnp.exp(jnp.full((NEAR, BLOCK), dust, F32)))
    total[...] = pot
    pots[...] = jnp.broadcast_to(pot[:, None, :], (NEAR, 8, BLOCK))
    copies = []
    for r in range(2):
        j = 2 * blk + r
        rows = lax.broadcasted_iota(jnp.int32, (BLOCK, BLOCK), 0) < kpt_ref[first + GROUP + j]
        for t in range(TILES):
            n = table(cov_ref, j, t)
            limit = jnp.where(t < table(cov_ref, j, TILES), kpt_ref[first + n], 0)
            full = base_ref[r * TILES + t].reshape(BLOCK // 8, 8, BLOCK) + pots[n][None]
            plan[r, t] = jnp.where(
                rows & (lanes((BLOCK, BLOCK)) < limit), full.reshape(BLOCK, BLOCK), 0.0
            )
            copy = pltpu.make_async_copy(
                plan.at[r, t], plan_hbm.at[r, t], sems.at[r * TILES + t]
            )
            copy.start()
            copies.append(copy)
        own = total[pl.ds(GROUP + j, 1), :]
        bin_ref[r : r + 1, :] = jnp.where(
            lanes((1, BLOCK)) < kpt_ref[first + GROUP + j], dust + own, 0.0
        )
    for copy in copies:
        copy.wait()


def swap_cores(x):
    count = lax.axis_size("blk")
    return lax.ppermute(x, "blk", [(b, b ^ 1) for b in range(count)])


def shifted(x, distance):
    count = lax.axis_size("img")
    route = [(i, i + distance) for i in range(count) if 0 <= i + distance < count]
    return lax.ppermute(x, "img", route)


def gather_near(copies):
    blks = lax.axis_size("blk")
    groups = [list(range(c, blks, 2)) for c in range(2)]
    own = lax.all_to_all(copies, "blk", 0, 0, tiled=True, axis_index_groups=groups)
    low = shifted(own, 1)
    high = shifted(own, -1)
    return own, swap_cores(own), low, swap_cores(low), high, swap_cores(high)


def exchange(m):
    imgs, blks = lax.axis_size("img"), lax.axis_size("blk")
    windows = []
    for b in range(blks):
        for i in range(2 * (b % 2), imgs + 2 * (b % 2), 4):
            windows.append([k % imgs * blks + b for k in range(i, i + 4)])
    x = lax.all_to_all(m, ("img", "blk"), 0, 0, tiled=True, axis_index_groups=windows)
    return x, swap_cores(x)


def call(kernel, ins, outs, scratch, limit):
    spaces = {"s": SMEM, "v": VMEM, "h": pl.ANY}
    out_specs = [pl.BlockSpec(memory_space=spaces[k]) for k, *_ in outs]
    return pl.pallas_call(
        kernel,
        in_specs=[pl.BlockSpec(memory_space=spaces[k]) for k, _ in ins],
        out_specs=out_specs,
        out_shape=[jax.ShapeDtypeStruct(s, d) for _, s, d in outs],
        scratch_shapes=scratch,
        compiler_params=pltpu.CompilerParams(vmem_limit_bytes=limit << 20),
    )(*[a for _, a in ins])


def on_device(
    descriptors, covisible, tile_counts, keypoints,
    query_weight, key_weight, value_weight, merge_weight, output_weight, dustbin,
):
    flat = descriptors.reshape(2 * BLOCK, D)
    (sent,) = call(
        pack_kernel,
        [("s", covisible), ("s", tile_counts), ("v", flat)],
        [("v", (4, CHUNK, D), BF)],
        [],
        4,
    )
    refined, lists = call(
        attend_kernel,
        [("s", covisible), ("s", tile_counts), ("s", keypoints), ("v", flat)]
        + [("v", a) for a in gather_near(sent)]
        + [("v", a) for a in (query_weight, key_weight, value_weight, merge_weight, output_weight)],
        [("v", (4, 2 * BLOCK, D), BF), ("v", (GROUP, BLOCK), jnp.int32)],
        [
            VMEM((2 * TILES * BLOCK, D), BF),
            VMEM((HEADS * BLOCK, TILES * BLOCK), F32),
            VMEM((HEADS * BLOCK, TILES * BLOCK), BF),
        ],
        24,
    )
    smem = [("s", lists), ("s", keypoints), ("s", dustbin)]
    sums = [("v", (NEAR, BLOCK), F32), ("v", (4, 2 * GROUP, BLOCK), F32)]
    tile = (BLOCK, BLOCK)
    summing = [VMEM((NEAR, 8, BLOCK), F32), VMEM((NEAR + GROUP, BLOCK), F32)]
    keep, top, own, s, m = call(
        build_kernel,
        smem + [("v", a) for a in gather_near(refined)],
        [("v", (GROUP * TILES, *tile), F32), ("v", (GROUP, *tile), F32), ("v", (2 * TILES, *tile), F32)]
        + sums,
        [VMEM((NEAR, BLOCK, D), BF), *summing, VMEM((TILES, *tile), F32)],
        24,
    )
    for sweep in range(1, ITERS):
        x, y = exchange(m)
        last = sweep == ITERS - 1
        more = [("v", (2 * TILES, *tile), F32), ("v", (2, BLOCK), F32)] if last else []
        got = call(
            functools.partial(sweep_kernel, last),
            smem + [("v", a) for a in (keep, top, own, s, x, y)],
            sums + more,
            [VMEM((NEAR, BLOCK), F32), VMEM((NEAR, 8, BLOCK), F32), *summing],
            16,
        )
        s, m = got[:2]
    base, row_bin = got[2:]
    x, y = exchange(m)
    plan, col_bin = call(
        plan_kernel,
        smem + [("v", a) for a in (base, s, x, y)],
        [("h", (2, TILES, *tile), F32), ("v", (2, BLOCK), F32)],
        [
            VMEM((NEAR, BLOCK), F32),
            VMEM((NEAR, 8, BLOCK), F32),
            VMEM((2, TILES, *tile), F32),
            pltpu.SemaphoreType.DMA((2 * TILES,)),
        ],
        16,
    )
    return plan, row_bin, col_bin


def solution(mesh):
    split = P(("img", "blk"))
    in_specs = (split, split, split, P(), P(), P(), P(), P(), P(), P())
    return jax.shard_map(
        on_device, mesh=mesh, in_specs=in_specs, out_specs=(split, split, split), check_vma=False
    )
```
